256 devices in a mesh: wide: 32 (over y_lo, z, core), narrow: 8 (over y_hi, x).
Axes of the slice: x: 4, y: 4 (y_hi: 2, y_lo: 2; y = y_hi * 2 + y_lo), z: 8, core: 2. Of those that a mesh axis runs over, the one named last changes fastest.
Arguments:
- tokens: bfloat16 [512, 16384], P('wide', 'narrow'), may hold values from -6 to 6
- gate_codes: bfloat16 [16384, 28672], P('narrow', 'wide'), may hold values from -6 to 6
- gate_scale: float32 [128, 224], P('narrow', 'wide'), may hold values from 0.00234375 to 0.0234375
- up_codes: bfloat16 [16384, 28672], P('narrow', 'wide'), may hold values from -6 to 6
- up_scale: float32 [128, 224], P('narrow', 'wide'), may hold values from 0.00234375 to 0.0234375
- down_codes: bfloat16 [28672, 16384], P('wide', 'narrow'), may hold values from -6 to 6
- down_scale: float32 [224, 128], P('wide', 'narrow'), may hold values from 0.0017717085 to 0.017717084
Outputs:
- mixed: bfloat16 [512, 16384], P('wide', 'narrow')
The draws below stay inside these ranges and needn't reach their ends.
All inputs are finite; a program needn't handle non-finite values.
Results may differ from the reference program's by a relative error of at most 0.03.
Values may be sent and summed in bfloat16 or wider, within the bound.
A program may use at most 64 MiB of HBM per device.

```python
import math
import jax
import jax.numpy as jnp
from jax import lax

D = 16384
FFW = 28672
BLOCK = 128
ROWS = 512


def levels(own_key, extent, pieces, smallest, largest):
    def one(axis_at, shards_of):
        steps = jax.random.uniform(jax.random.fold_in(jax.random.fold_in(own_key, 6), axis_at), (shards_of,), jnp.float32, smallest / len(pieces), largest / len(pieces))
        return jnp.repeat(jnp.exp(steps), extent[axis_at] // shards_of).reshape((-1,) + (1,) * (len(extent) - axis_at - 1))

    gain = one(*pieces[0])
    for cut in pieces[1:]:
        gain = gain * one(*cut)
    return gain


def scatter_about(key, shape, deviation, most, cuts=(), kind=jnp.bfloat16):
    factor_of = levels(key, shape, cuts, -0.22, 0.18) if cuts else 1.0
    entries = jax.random.normal(key, shape, jnp.float32) * deviation * factor_of
    return jnp.minimum(jnp.maximum(entries, -most), most).astype(kind)


def setup_inputs(seed: int = 0) -> dict:
    key_list = jax.random.split(jax.random.key(seed), 8)
    tokens = scatter_about(key_list[0], (ROWS, D), 1.0, 6.0, ((0, 32), (1, 8)))
    gate_codes = scatter_about(key_list[1], (D, FFW), 1.0, 6.0, ((0, 8), (1, 32)))
    gate_scale = jnp.clip(jnp.exp(math.log(0.0234375) - 2.3025851 * jax.random.uniform(key_list[2], (D // BLOCK, FFW // BLOCK), jnp.float32) ** levels(key_list[2], (D // BLOCK, FFW // BLOCK), ((0, 8), (1, 32)), -0.2, 0.2)), 0.00234375, 0.0234375)
    up_codes = scatter_about(key_list[3], (D, FFW), 1.0, 6.0, ((0, 8), (1, 32)))
    up_scale = jnp.clip(jnp.exp(math.log(0.0234375) - 2.3025851 * jax.random.uniform(key_list[4], (D // BLOCK, FFW // BLOCK), jnp.float32) ** levels(key_list[4], (D // BLOCK, FFW // BLOCK), ((0, 8), (1, 32)), -0.2, 0.2)), 0.00234375, 0.0234375)
    down_codes = scatter_about(key_list[5], (FFW, D), 1.0, 6.0, ((0, 32), (1, 8)))
    down_scale = jnp.clip(jnp.exp(math.log(0.017717084) - 2.30258504 * jax.random.uniform(key_list[6], (FFW // BLOCK, D // BLOCK), jnp.float32) ** levels(key_list[6], (FFW // BLOCK, D // BLOCK), ((0, 32), (1, 8)), -0.2, 0.2)), 0.0017717085, 0.017717084)
    return {"tokens": tokens, "gate_codes": gate_codes, "gate_scale": gate_scale, "up_codes": up_codes, "up_scale": up_scale, "down_codes": down_codes, "down_scale": down_scale}


def reference(tokens, gate_codes, gate_scale, up_codes, up_scale, down_codes, down_scale):
    def column_block(codes, scale, index):
        cols = lax.dynamic_slice_in_dim(codes, index * BLOCK, BLOCK, 1)
        factor = jnp.repeat(lax.dynamic_slice_in_dim(scale, index, 1, 1), BLOCK, axis=0)
        return (cols.astype(jnp.float32) * factor).astype(jnp.bfloat16)

    def step(index, total):
        gate_weight = column_block(gate_codes, gate_scale, index)
        up_weight = column_block(up_codes, up_scale, index)
        rows_block = lax.dynamic_slice_in_dim(down_codes, index * BLOCK, BLOCK, 0)
        factor = jnp.repeat(lax.dynamic_slice_in_dim(down_scale, index, 1, 0), BLOCK, axis=1)
        down_weight = (rows_block.astype(jnp.float32) * factor).astype(jnp.bfloat16)
        gate = jnp.dot(tokens, gate_weight, preferred_element_type=jnp.float32)
        up = jnp.dot(tokens, up_weight, preferred_element_type=jnp.float32)
        hidden = (jax.nn.silu(gate) * up).astype(jnp.bfloat16)
        return total + jnp.dot(hidden, down_weight, preferred_element_type=jnp.float32)

    start = jnp.zeros((tokens.shape[0], tokens.shape[1]), jnp.float32)
    total = lax.fori_loop(0, FFW // BLOCK, step, start)
    return total.astype(jnp.bfloat16)
```

```python
import functools

import jax
import jax.numpy as jnp
from jax import lax
from jax.experimental import pallas as pl
from jax.experimental.pallas import tpu as pltpu
from jax.sharding import PartitionSpec as P

MESH = pl.DeviceIdType.MESH
BLOCK = 128
TILE = 256
SHARD = 16
OFFSETS = (0, -1, 1, -2, 2, -3, 3, 4)
HALF = 256


def place():
    wide, narrow = lax.axis_index("wide"), lax.axis_index("narrow")
    return wide // 16, (wide // 2) % 8, wide % 2, narrow // 4, narrow % 4


def kernel(
    tokens, gate_codes, gate_scale, up_codes, up_scale, down_codes, down_scale,
    mixed,
    gate_in, up_in, down_in, weight, down, rows, sums, hidden, outs,
    send1, send2, send3, recv1, recv2, recv3,
    core_send, core_recv, side_send, side_recv, ring_send, ring_recv,
    load_sem, a_send, az_recv, ay_recv, ac_recv,
    b_send, b_recv, c_send, c_recv, d_send, d_recv, e_send, e_recv,
):
    y_lo, z, core, y_hi, x = place()
    units = gate_codes.shape[1]
    b1 = ((x + 1) // 2) % 2
    b2 = x // 2
    narrow = y_hi * 4 + x
    wide = y_lo * 16 + z * 2 + core

    def at_z(step):
        return (y_lo * 16 + ((z + step + 8) % 8) * 2 + core, narrow)

    side = ((1 - y_lo) * 16 + z * 2 + core, narrow)
    twin = (y_lo * 16 + z * 2 + 1 - core, narrow)
    first = (wide, y_hi * 4 + x + 1 - 2 * (x % 2))
    second = (wide, y_hi * 4 + 3 - x)
    across = (wide, (1 - y_hi) * 4 + x)

    loads = []
    for index, (source, target) in enumerate(
        ((gate_codes, gate_in), (up_codes, up_in), (down_codes, down_in))
    ):
        loads.append(pltpu.make_async_copy(source, target, load_sem.at[index]))
    own = pltpu.make_async_copy(tokens, rows.at[0, 0, 0, 0], load_sem.at[3])
    own.start()
    for load in loads:
        load.start()

    barrier = pltpu.get_barrier_semaphore()
    partners = [at_z(step) for step in OFFSETS[1:]] + [side, twin, first, second, across]
    for partner in partners:
        pl.semaphore_signal(barrier, inc=1, device_id=partner, device_id_type=MESH)
    pl.semaphore_wait(barrier, len(partners))

    def remote(source, target, send_sem, recv_sem, device):
        copy = pltpu.make_async_remote_copy(
            src_ref=source, dst_ref=target, send_sem=send_sem, recv_sem=recv_sem,
            device_id=device, device_id_type=MESH,
        )
        copy.start()
        return copy

    def shard(slot, other_core, other_side):
        return rows.at[slot // 4, other_core, slot % 4, other_side]

    z_copies, y_copies, c_copies = {}, {}, {}

    def z_send(source, slot, step, columns=None):
        index = slot if columns is None else 7 + columns
        target = shard(slot, 0, 0)
        if columns is not None:
            width = target.shape[1] // 2
            cut = pl.ds(columns * width, width)
            source, target = source.at[:, cut], target.at[:, cut]
        z_copies[index] = remote(source, target, a_send.at[index], az_recv.at[index], at_z(step))

    def y_send(source, slot):
        y_copies[slot] = remote(
            source, shard(slot, 0, 1), a_send.at[9 + slot], ay_recv.at[slot], side
        )

    def c_send_(source, slot, other_side):
        index = slot * 2 + other_side
        c_copies[index] = remote(
            source, shard(slot, 1, other_side), a_send.at[17 + index], ac_recv.at[index], twin
        )

    def spread(slot):
        y_send(shard(slot, 0, 0), slot)
        c_send_(shard(slot, 0, 0), slot, 0)

    def relay(slot):
        y_copies[slot].wait_recv()
        c_send_(shard(slot, 0, 1), slot, 1)

    def widen(step, _):
        span = pl.ds(pl.multiple_of(step * BLOCK, BLOCK), BLOCK)
        for half, (codes, scale) in enumerate(((gate_in, gate_scale), (up_in, up_scale))):
            for col in range(units // BLOCK):
                cut = slice(col * BLOCK, (col + 1) * BLOCK)
                block = codes[span, cut].astype(jnp.float32) * scale[step, col]
                to = slice(half * units + col * BLOCK, half * units + (col + 1) * BLOCK)
                weight[span, to] = block.astype(jnp.bfloat16)
        return 0

    def widen_down(step, _):
        span = pl.ds(pl.multiple_of(step * BLOCK, BLOCK), BLOCK)
        for col in range(down.shape[1] // BLOCK):
            cut = slice(col * BLOCK, (col + 1) * BLOCK)
            block = down_in[span, cut].astype(jnp.float32) * down_scale[step, col]
            down[span, cut] = block.astype(jnp.bfloat16)
        return 0

    z_send(tokens, 1, 1)
    z_send(tokens, 2, -1)
    y_send(tokens, 0)
    c_send_(tokens, 0, 0)
    loads[0].wait()
    loads[1].wait()
    steps = weight.shape[0] // BLOCK
    lax.fori_loop(0, steps // 4, widen, 0)
    z_copies[1].wait_recv()
    z_send(shard(1, 0, 0), 3, 1)
    spread(1)
    z_copies[2].wait_recv()
    z_send(shard(2, 0, 0), 4, -1)
    spread(2)
    relay(0)
    lax.fori_loop(steps // 4, steps // 2, widen, 0)
    z_copies[3].wait_recv()
    z_send(shard(3, 0, 0), 5, 1)
    spread(3)
    z_copies[4].wait_recv()
    z_send(shard(4, 0, 0), 6, -1)
    spread(4)
    relay(1)
    relay(2)
    lax.fori_loop(steps // 2, steps, widen, 0)
    z_copies[5].wait_recv()
    z_send(shard(5, 0, 0), 7, 1, 0)
    spread(5)
    z_copies[6].wait_recv()
    z_send(shard(6, 0, 0), 7, -1, 1)
    spread(6)
    relay(3)

    def multiply(chunk):
        left = rows.at[chunk].reshape(HALF, rows.shape[-1])

        def tile(step, _):
            cut = pl.ds(pl.multiple_of(step * TILE, TILE), TILE)
            sums[pl.ds(chunk * HALF, HALF), cut] = jnp.dot(
                left[...], weight[:, cut], preferred_element_type=jnp.float32
            )
            return 0

        lax.fori_loop(0, weight.shape[1] // TILE, tile, 0)

    lead, follow = (b1, b2), (b2, b1)
    lead_to, follow_to = (first, second), (second, first)
    copies1, copies2, copies3 = {}, {}, {}

    def base(chunk, stream):
        return chunk * HALF + stream * (HALF // 2)

    def span(start, size):
        return pl.ds(pl.multiple_of(start, SHARD), size)

    def scatter1(chunk):
        for stream in range(2):
            at = chunk * 2 + stream
            away = base(chunk, stream) + (1 - lead[stream]) * 64
            send1[at] = sums[span(away, 64), :].astype(jnp.bfloat16)
            copies1[at] = remote(
                send1.at[at], recv1.at[at], b_send.at[at], b_recv.at[at], lead_to[stream]
            )

    def scatter2(chunk):
        for stream in range(2):
            at = chunk * 2 + stream
            copies1[at].wait_recv()
            away = (1 - follow[stream]) * 32
            start = base(chunk, stream) + lead[stream] * 64 + away
            send2[at] = (
                sums[span(start, 32), :] + recv1[at, span(away, 32), :].astype(jnp.float32)
            ).astype(jnp.bfloat16)
            copies2[at] = remote(
                send2.at[at], recv2.at[at], b_send.at[4 + at], b_recv.at[4 + at], follow_to[stream]
            )

    def scatter3(chunk):
        for stream in range(2):
            at = chunk * 2 + stream
            copies2[at].wait_recv()
            away = (1 - y_hi) * SHARD
            inner = follow[stream] * 32 + away
            start = base(chunk, stream) + lead[stream] * 64 + inner
            send3[at] = (
                sums[span(start, SHARD), :]
                + recv1[at, span(inner, SHARD), :].astype(jnp.float32)
                + recv2[at, span(away, SHARD), :].astype(jnp.float32)
            ).astype(jnp.bfloat16)
            copies3[at] = remote(
                send3.at[at], recv3.at[at], b_send.at[8 + at], b_recv.at[8 + at], across
            )

    def mine(chunk, stream):
        return base(chunk, stream) + lead[stream] * 64 + follow[stream] * 32 + y_hi * SHARD

    gathers = {}

    def gather(chunk, stream, stage, start, size, device):
        index = stage * 4 + chunk * 2 + stream
        piece = hidden.at[span(start, size)]
        gathers[stage, chunk, stream] = remote(
            piece, piece, c_send.at[index], c_recv.at[index], device
        )

    def activate(chunk):
        for stream in range(2):
            at = chunk * 2 + stream
            copies3[at].wait_recv()
            inner = follow[stream] * 32 + y_hi * SHARD
            total = (
                sums[span(mine(chunk, stream), SHARD), :]
                + recv1[at, span(inner, SHARD), :].astype(jnp.float32)
                + recv2[at, span(y_hi * SHARD, SHARD), :].astype(jnp.float32)
                + recv3[at].astype(jnp.float32)
            )
            gate, up = total[:, :units], total[:, units:]
            hidden[span(mine(chunk, stream), SHARD), :] = (
                gate / (1.0 + jnp.exp(-gate)) * up
            ).astype(jnp.bfloat16)
            gather(chunk, stream, 0, mine(chunk, stream), SHARD, across)

    def gather2(chunk):
        for stream in range(2):
            gathers[0, chunk, stream].wait_recv()
            start = base(chunk, stream) + lead[stream] * 64 + follow[stream] * 32
            gather(chunk, stream, 1, start, 32, follow_to[stream])

    def gather3(chunk):
        for stream in range(2):
            gathers[1, chunk, stream].wait_recv()
            gather(chunk, stream, 2, base(chunk, stream) + lead[stream] * 64, 64, lead_to[stream])

    twins, sides, rings = {}, {}, {}

    def project(chunk):
        for stream in range(2):
            gathers[2, chunk, stream].wait_recv()

        def tile(step, _):
            cut = pl.ds(pl.multiple_of(step * TILE, TILE), TILE)
            outs[chunk, :, cut] = jnp.dot(
                hidden[pl.ds(chunk * HALF, HALF), :], down[:, cut],
                preferred_element_type=jnp.float32,
            )
            return 0

        lax.fori_loop(0, down.shape[1] // TILE, tile, 0)
        core_send[chunk] = outs[chunk, HALF // 2 :, :].astype(jnp.bfloat16)
        twins[chunk] = remote(
            core_send.at[chunk], core_recv.at[chunk], d_send.at[chunk], d_recv.at[chunk], twin
        )

    def to_side(chunk):
        twins[chunk].wait_recv()
        for slot in range(4):
            away = pl.ds(slot * 32 + SHARD, SHARD)
            side_send[chunk, slot] = (
                outs[chunk, away, :] + core_recv[chunk, away, :].astype(jnp.float32)
            ).astype(jnp.bfloat16)
        sides[chunk] = remote(
            side_send.at[chunk], side_recv.at[chunk],
            d_send.at[2 + chunk], d_recv.at[2 + chunk], side,
        )

    def local(slot):
        chunk, near = slot // 4, pl.ds((slot % 4) * 32, SHARD)
        return (
            outs[chunk, near, :]
            + core_recv[chunk, near, :].astype(jnp.float32)
            + side_recv[chunk, slot % 4].astype(jnp.float32)
        )

    def to_ring(chunk):
        sides[chunk].wait_recv()
        for slot in range(chunk * 4, chunk * 4 + 4):
            if slot > 0:
                ring_send[slot - 1] = local(slot).astype(jnp.bfloat16)
                rings[slot] = remote(
                    ring_send.at[slot - 1], ring_recv.at[slot - 1],
                    e_send.at[slot - 1], e_recv.at[slot - 1], at_z(OFFSETS[slot]),
                )

    own.wait()
    for index in range(8):
        c_copies[index].wait_recv()
    multiply(0)
    scatter1(0)
    z_copies[7].wait_recv()
    z_copies[8].wait_recv()
    spread(7)
    for slot in range(4, 8):
        relay(slot)
    for index in range(8, 16):
        c_copies[index].wait_recv()
    multiply(1)
    scatter1(1)
    loads[2].wait()
    lax.fori_loop(0, down.shape[0] // BLOCK, widen_down, 0)
    scatter2(0)
    scatter3(0)
    scatter2(1)
    activate(0)
    scatter3(1)
    gather2(0)
    activate(1)
    gather3(0)
    gather2(1)
    project(0)
    gather3(1)
    to_side(0)
    to_ring(0)
    project(1)
    to_side(1)
    to_ring(1)
    total = local(0)
    for slot in range(1, 8):
        rings[slot].wait_recv()
        total = total + ring_recv[slot - 1].astype(jnp.float32)
    mixed[...] = total.astype(jnp.bfloat16)

    groups = (z_copies, y_copies, c_copies, copies1, copies2, copies3, gathers, twins, sides, rings)
    for group in groups:
        for copy in group.values():
            copy.wait_send()


def feed_forward(tokens, gate_codes, gate_scale, up_codes, up_scale, down_codes, down_scale):
    depth, units = gate_codes.shape
    bf16, f32 = jnp.bfloat16, jnp.float32
    any_space, scalars = pl.BlockSpec(memory_space=pl.ANY), pl.BlockSpec(memory_space=pltpu.SMEM)
    dma = pltpu.SemaphoreType.DMA
    return pl.pallas_call(
        kernel,
        out_shape=jax.ShapeDtypeStruct(tokens.shape, bf16),
        in_specs=[any_space, any_space, scalars, any_space, scalars, any_space, scalars],
        out_specs=pl.BlockSpec(memory_space=pltpu.VMEM),
        scratch_shapes=[
            pltpu.VMEM((depth, units), bf16),
            pltpu.VMEM((depth, units), bf16),
            pltpu.VMEM((units, depth), bf16),
            pltpu.VMEM((depth, 2 * units), bf16),
            pltpu.VMEM((units, depth), bf16),
            pltpu.VMEM((2, 2, 4, 2, SHARD, depth), bf16),
            pltpu.VMEM((2 * HALF, 2 * units), f32),
            pltpu.VMEM((2 * HALF, units), bf16),
            pltpu.VMEM((2, HALF, depth), f32),
            pltpu.VMEM((4, 64, 2 * units), bf16),
            pltpu.VMEM((4, 32, 2 * units), bf16),
            pltpu.VMEM((4, SHARD, 2 * units), bf16),
            pltpu.VMEM((4, 64, 2 * units), bf16),
            pltpu.VMEM((4, 32, 2 * units), bf16),
            pltpu.VMEM((4, SHARD, 2 * units), bf16),
            pltpu.VMEM((2, HALF // 2, depth), bf16),
            pltpu.VMEM((2, HALF // 2, depth), bf16),
            pltpu.VMEM((2, 4, SHARD, depth), bf16),
            pltpu.VMEM((2, 4, SHARD, depth), bf16),
            pltpu.VMEM((7, SHARD, depth), bf16),
            pltpu.VMEM((7, SHARD, depth), bf16),
            dma((4,)),
            dma((33,)),
            dma((9,)),
            dma((8,)),
            dma((16,)),
            dma((12,)),
            dma((12,)),
            dma((12,)),
            dma((12,)),
            dma((4,)),
            dma((4,)),
            dma((7,)),
            dma((7,)),
        ],
        compiler_params=pltpu.CompilerParams(
            collective_id=0, has_side_effects=True, vmem_limit_bytes=56 << 20
        ),
    )(tokens, gate_codes, gate_scale, up_codes, up_scale, down_codes, down_scale)


def solution(mesh):
    return jax.shard_map(
        feed_forward,
        mesh=mesh,
        in_specs=(
            P("wide", "narrow"),
            P("narrow", "wide"),
            P("narrow", "wide"),
            P("narrow", "wide"),
            P("narrow", "wide"),
            P("wide", "narrow"),
            P("wide", "narrow"),
        ),
        out_specs=P("wide", "narrow"),
        check_vma=False,
    )
```

```python
import jax
import jax.numpy as jnp
from jax import lax
from jax.experimental import pallas as pl
from jax.experimental.pallas import tpu as pltpu
from jax.sharding import PartitionSpec as P

MESH = pl.DeviceIdType.MESH
BLOCK = 128
TILE = 256
SHARD = 16
UNITS = 4
UNIT = 128
QUARTER = 64
COPIES = 128
OFFSETS = (1, -1, 3, -3, 4, 0, 2, -2)


def kernel(
    tokens, gate_codes, gate_scale, up_codes, up_scale, down_codes, down_scale,
    mixed,
    gate_in, up_in, down_in, weight, down, rows, sums, hidden, outs,
    send1, send2, recv1, recv2,
    core_send, core_recv, side_send, side_recv, ring_send, ring_recv, last_send, last_recv,
    load_sem, send_sem, recv_sem,
):
    wide, narrow = lax.axis_index("wide"), lax.axis_index("narrow")
    y_lo, z, core, y_hi, x = wide // 16, (wide // 2) % 8, wide % 2, narrow // 4, narrow % 4
    units = gate_codes.shape[1]

    def at_z(step, other_side=0):
        y = 1 - y_lo if other_side else y_lo
        return (y * 16 + ((z + step + 8) % 8) * 2 + core, narrow)

    side = ((1 - y_lo) * 16 + z * 2 + core, narrow)
    twin = (y_lo * 16 + z * 2 + 1 - core, narrow)
    first_x, second_x = x + 1 - 2 * (x % 2), 3 - x
    bits = (((x + 1) // 2) % 2, x // 2)
    pairs = ((wide, y_hi * 4 + first_x), (wide, y_hi * 4 + second_x))
    across = (wide, (1 - y_hi) * 4 + x)
    diagonals = ((wide, (1 - y_hi) * 4 + first_x), (wide, (1 - y_hi) * 4 + second_x))

    loads = [
        pltpu.make_async_copy(source, target, load_sem.at[index])
        for index, (source, target) in enumerate(
            (
                (tokens, rows.at[OFFSETS.index(0) // 2, 0, OFFSETS.index(0) % 2, 0]),
                (gate_codes, gate_in),
                (up_codes, up_in),
                (down_codes, down_in),
            )
        )
    ]
    for load in loads:
        load.start()

    barrier = pltpu.get_barrier_semaphore()
    partners = [at_z(step) for step in OFFSETS if step] + [at_z(2, 1), at_z(-2, 1)]
    partners += [side, twin, across, *pairs, *diagonals]
    for partner in partners:
        pl.semaphore_signal(barrier, inc=1, device_id=partner, device_id_type=MESH)
    pl.semaphore_wait(barrier, len(partners))

    started = []

    def remote(source, target, device):
        index = len(started)
        copy = pltpu.make_async_remote_copy(
            src_ref=source, dst_ref=target,
            send_sem=send_sem.at[index], recv_sem=recv_sem.at[index],
            device_id=device, device_id_type=MESH,
        )
        copy.start()
        started.append(copy)
        return copy

    def shard(offset, other_core, other_side):
        slot = OFFSETS.index(offset)
        return rows.at[slot // 2, other_core, slot % 2, other_side]

    arrivals = {}

    def to_twin(offset, other_side):
        arrivals[offset, 1, other_side] = remote(
            shard(offset, 0, other_side), shard(offset, 1, other_side), twin
        )

    def to_other_side(offset):
        arrivals[offset, 0, 1] = [remote(shard(offset, 0, 0), shard(offset, 0, 1), side)]

    def take(offset, other_side):
        for copy in arrivals[offset, 0, other_side]:
            copy.wait_recv()
        to_twin(offset, other_side)

    middle = BLOCK * ((units // BLOCK + 1) // 2)
    streams = ((0, middle), (middle, units))

    def both(stream):
        start, end = streams[stream]
        return pl.ds(2 * start, 2 * (end - start))

    def widen(step, _):
        span = pl.ds(pl.multiple_of(step * BLOCK, BLOCK), BLOCK)
        for second, (codes, scale) in enumerate(((gate_in, gate_scale), (up_in, up_scale))):
            for start, end in streams:
                for at in range(start, end, BLOCK):
                    block = codes[span, at : at + BLOCK].astype(jnp.float32) * scale[at // BLOCK, step]
                    to = start + at + second * (end - start)
                    weight[span, to : to + BLOCK] = block.astype(jnp.bfloat16)
        return 0

    def widen_down(step, _):
        span = pl.ds(pl.multiple_of(step * BLOCK, BLOCK), BLOCK)
        for col in range(down.shape[1] // BLOCK):
            cut = slice(col * BLOCK, (col + 1) * BLOCK)
            block = down_in[span, cut].astype(jnp.float32) * down_scale[step, col]
            down[span, cut] = block.astype(jnp.bfloat16)
        return 0

    def span(start, size):
        return pl.ds(pl.multiple_of(start, SHARD), size)

    def lead(unit, stream):
        return (unit + stream) % 2

    def base(unit, stream):
        return unit * UNIT + bits[lead(unit, stream)] * QUARTER

    def within(unit, stream, other_x, other_y):
        follow = bits[1 - lead(unit, stream)]
        return (1 - follow if other_x else follow) * 32 + (1 - y_hi if other_y else y_hi) * SHARD

    def trio(unit, stream):
        follow = 1 - lead(unit, stream)
        return ((1, 0, pairs[follow]), (0, 1, across), (1, 1, diagonals[follow]))

    halves, quarters, gathers, forwards = {}, {}, {}, {}

    def multiply(unit):
        for offset in OFFSETS[2 * unit : 2 * unit + 2]:
            arrivals[offset, 1, 0].wait_recv()
            arrivals[offset, 1, 1].wait_recv()

        def tile(step, _):
            cut = pl.ds(pl.multiple_of(step * TILE, TILE), TILE)
            left = rows[unit].reshape(UNIT, rows.shape[-1])
            sums[pl.ds(unit * UNIT, UNIT), cut] = jnp.dot(
                left, weight[:, cut], preferred_element_type=jnp.float32
            )
            return 0

        for stream, (start, end) in enumerate(streams):
            lax.fori_loop(2 * start // TILE, 2 * end // TILE, tile, 0)
            away = unit * UNIT + (1 - bits[lead(unit, stream)]) * QUARTER
            cut = both(stream)
            send1[unit, :, cut] = sums[span(away, QUARTER), cut].astype(jnp.bfloat16)
            halves[unit, stream] = remote(
                send1.at[unit, :, cut], recv1.at[unit, :, cut], pairs[lead(unit, stream)]
            )

    def partial(unit, stream, other_x, other_y):
        inner, cut = within(unit, stream, other_x, other_y), both(stream)
        return sums[span(base(unit, stream) + inner, SHARD), cut] + recv1[
            unit, span(inner, SHARD), cut
        ].astype(jnp.float32)

    def scatter(unit):
        for stream in range(2):
            halves[unit, stream].wait_recv()
            cut = both(stream)
            for index, (other_x, other_y, device) in enumerate(trio(unit, stream)):
                send2[unit, index, :, cut] = partial(unit, stream, other_x, other_y).astype(
                    jnp.bfloat16
                )
                quarters[unit, stream, index] = remote(
                    send2.at[unit, index, :, cut], recv2.at[unit, index, :, cut], device
                )

    def activate(unit):
        for stream, (start, end) in enumerate(streams):
            total = partial(unit, stream, 0, 0)
            for index in range(3):
                quarters[unit, stream, index].wait_recv()
                total = total + recv2[unit, index, :, both(stream)].astype(jnp.float32)
            gate, up = total[:, : end - start], total[:, end - start :]
            mine = span(base(unit, stream) + within(unit, stream, 0, 0), SHARD)
            hidden[mine, start:end] = (gate / (1.0 + jnp.exp(-gate)) * up).astype(jnp.bfloat16)
            piece = hidden.at[mine, pl.ds(start, end - start)]
            for index, (_, _, device) in enumerate(trio(unit, stream)):
                gathers[unit, stream, index] = remote(piece, piece, device)

    def forward(unit):
        for stream, (start, end) in enumerate(streams):
            for index in range(3):
                gathers[unit, stream, index].wait_recv()
            piece = hidden.at[span(base(unit, stream), QUARTER), pl.ds(start, end - start)]
            forwards[unit, stream] = remote(piece, piece, pairs[lead(unit, stream)])

    twins, sides, rings, lasts, folded = {}, {}, {}, {}, []

    def project(unit):
        for stream in range(2):
            forwards[unit, stream].wait_recv()

        def tile(step, _):
            cut = pl.ds(pl.multiple_of(step * TILE, TILE), TILE)
            outs[unit, :, cut] = jnp.dot(
                hidden[pl.ds(unit * UNIT, UNIT), :], down[:, cut],
                preferred_element_type=jnp.float32,
            )
            return 0

        lax.fori_loop(0, down.shape[1] // TILE, tile, 0)
        core_send[unit] = outs[unit, QUARTER:, :].astype(jnp.bfloat16)
        twins[unit] = remote(core_send.at[unit], core_recv.at[unit], twin)

    def paired(slot, other_side):
        at = pl.ds((slot % 2) * 32 + other_side * SHARD, SHARD)
        return outs[slot // 2, at, :] + core_recv[slot // 2, at, :].astype(jnp.float32)

    def to_side(unit):
        twins[unit].wait_recv()
        for slot in (2 * unit, 2 * unit + 1):
            side_send[slot] = paired(slot, 1).astype(jnp.bfloat16)
        cut = pl.ds(2 * unit, 2)
        sides[unit] = remote(side_send.at[cut], side_recv.at[cut], side)

    def local(slot):
        return paired(slot, 0) + side_recv[slot].astype(jnp.float32)

    def to_ring(unit):
        sides[unit].wait_recv()
        for slot in (2 * unit, 2 * unit + 1):
            folded.append(slot)
            if OFFSETS[slot]:
                ring_send[slot] = local(slot).astype(jnp.bfloat16)
                rings[slot] = remote(ring_send.at[slot], ring_recv.at[slot], at_z(OFFSETS[slot]))

    def straight(unit):
        twins[unit].wait_recv()
        for slot in (2 * unit, 2 * unit + 1):
            for other_side in range(2):
                if OFFSETS[slot] or other_side:
                    index = (slot % 2) * 2 + other_side
                    last_send[index] = paired(slot, other_side).astype(jnp.bfloat16)
                    lasts[index] = remote(
                        last_send.at[index], last_recv.at[index], at_z(OFFSETS[slot], other_side)
                    )

    loads[0].wait()
    for offset in (1, -1):
        arrivals[offset, 0, 0] = [remote(shard(0, 0, 0), shard(offset, 0, 0), at_z(-offset))]
    to_other_side(0)
    for offset in (2, -2):
        arrivals[offset, 0, 0] = [remote(shard(0, 0, 0), shard(offset, 0, 0), at_z(-offset))]
    to_twin(0, 0)
    arrivals[4, 0, 0] = []
    steps = weight.shape[0] // BLOCK
    loads[1].wait()
    loads[2].wait()
    lax.fori_loop(0, steps // 4, widen, 0)
    take(0, 1)
    for offset in (1, -1):
        arrivals[offset, 0, 1] = [remote(shard(0, 0, 1), shard(offset, 0, 1), at_z(-offset))]
    take(1, 0)
    take(-1, 0)
    lax.fori_loop(steps // 4, steps // 2, widen, 0)
    half = tokens.shape[1] // 2
    for offset, sign, columns in ((2, 1, pl.ds(0, half)), (-2, -1, pl.ds(half, half))):
        take(offset, 0)
        here = shard(offset, 0, 0)
        arrivals[3 * sign, 0, 0] = [remote(here, shard(3 * sign, 0, 0), at_z(-sign))]
        arrivals[4, 0, 0].append(
            remote(here.at[:, columns], shard(4, 0, 0).at[:, columns], at_z(-2 * sign))
        )
        to_other_side(offset)
    lax.fori_loop(steps // 2, steps, widen, 0)
    take(1, 1)
    take(-1, 1)
    multiply(0)
    take(3, 0)
    to_other_side(3)
    take(2, 1)
    take(-3, 0)
    to_other_side(-3)
    take(-2, 1)
    take(4, 0)
    to_other_side(4)
    multiply(3)
    take(3, 1)
    take(-3, 1)
    loads[3].wait()
    lax.fori_loop(0, down.shape[0] // BLOCK, widen_down, 0)
    scatter(0)
    multiply(1)
    take(4, 1)
    scatter(3)
    multiply(2)
    activate(0)
    scatter(1)
    activate(3)
    scatter(2)
    forward(0)
    activate(1)
    forward(3)
    project(0)
    activate(2)
    to_side(0)
    forward(1)
    project(3)
    to_side(3)
    forward(2)
    project(1)
    to_ring(0)
    to_side(1)
    project(2)
    to_ring(3)
    to_side(2)
    to_ring(1)
    to_ring(2)
    total = paired(OFFSETS.index(0), 0)
    if OFFSETS.index(0) in folded:
        total = local(OFFSETS.index(0))
    for slot, copy in rings.items():
        copy.wait_recv()
        total = total + ring_recv[slot].astype(jnp.float32)
    for index, copy in lasts.items():
        copy.wait_recv()
        total = total + last_recv[index].astype(jnp.float32)
    mixed[...] = total.astype(jnp.bfloat16)

    for copy in started:
        copy.wait_send()


def feed_forward(tokens, gate_codes, gate_scale, up_codes, up_scale, down_codes, down_scale):
    depth, units = gate_codes.shape
    bf16, f32 = jnp.bfloat16, jnp.float32
    any_space, scalars = pl.BlockSpec(memory_space=pl.ANY), pl.BlockSpec(memory_space=pltpu.SMEM)
    dma = pltpu.SemaphoreType.DMA
    return pl.pallas_call(
        kernel,
        out_shape=jax.ShapeDtypeStruct(tokens.shape, bf16),
        in_specs=[any_space, any_space, scalars, any_space, scalars, any_space, scalars],
        out_specs=pl.BlockSpec(memory_space=pltpu.VMEM),
        scratch_shapes=[
            pltpu.VMEM((depth, units), bf16),
            pltpu.VMEM((depth, units), bf16),
            pltpu.VMEM((units, depth), bf16),
            pltpu.VMEM((depth, 2 * units), bf16),
            pltpu.VMEM((units, depth), bf16),
            pltpu.VMEM((UNITS, 2, 2, 2, SHARD, depth), bf16),
            pltpu.VMEM((UNITS * UNIT, 2 * units), f32),
            pltpu.VMEM((UNITS * UNIT, units), bf16),
            pltpu.VMEM((UNITS, UNIT, depth), f32),
            pltpu.VMEM((UNITS, QUARTER, 2 * units), bf16),
            pltpu.VMEM((UNITS, 3, SHARD, 2 * units), bf16),
            pltpu.VMEM((UNITS, QUARTER, 2 * units), bf16),
            pltpu.VMEM((UNITS, 3, SHARD, 2 * units), bf16),
            pltpu.VMEM((UNITS, QUARTER, depth), bf16),
            pltpu.VMEM((UNITS, QUARTER, depth), bf16),
            pltpu.VMEM((2 * UNITS, SHARD, depth), bf16),
            pltpu.VMEM((2 * UNITS, SHARD, depth), bf16),
            pltpu.VMEM((2 * UNITS, SHARD, depth), bf16),
            pltpu.VMEM((2 * UNITS, SHARD, depth), bf16),
            pltpu.VMEM((4, SHARD, depth), bf16),
            pltpu.VMEM((4, SHARD, depth), bf16),
            dma((4,)),
            dma((COPIES,)),
            dma((COPIES,)),
        ],
        compiler_params=pltpu.CompilerParams(
            collective_id=0, has_side_effects=True, vmem_limit_bytes=56 << 20
        ),
    )(tokens, gate_codes, gate_scale.T, up_codes, up_scale.T, down_codes, down_scale)


def solution(mesh):
    return jax.shard_map(
        feed_forward,
        mesh=mesh,
        in_specs=(
            P("wide", "narrow"),
            P("narrow", "wide"),
            P("narrow", "wide"),
            P("narrow", "wide"),
            P("narrow", "wide"),
            P("wide", "narrow"),
            P("wide", "narrow"),
        ),
        out_specs=P("wide", "narrow"),
        check_vma=False,
    )
```

```python
import jax
import jax.numpy as jnp
from jax import lax
from jax.experimental import pallas as pl
from jax.experimental.pallas import tpu as pltpu
from jax.sharding import PartitionSpec as P

MESH = pl.DeviceIdType.MESH
BLOCK = 128
SHARD = 16
UNITS = 4
UNIT = 128
QUARTER = 64
COPIES = 128
OFFSETS = (1, -1, 3, -3, 4, 0, 2, -2)


def kernel(
    tokens, gate_codes, gate_scale, up_codes, up_scale, down_codes, down_scale,
    mixed,
    gate_in, up_in, down_in, weight, down, rows, sums, hidden, outs,
    send1, send2, recv1, recv2,
    core_send, core_recv, side_send, side_recv, ring_send, ring_recv,
    load_sem, send_sem, recv_sem,
):
    wide, narrow = lax.axis_index("wide"), lax.axis_index("narrow")
    y_lo, z, core, y_hi, x = wide // 16, (wide // 2) % 8, wide % 2, narrow // 4, narrow % 4
    units = gate_codes.shape[1]

    def at_z(step):
        return (y_lo * 16 + ((z + step + 8) % 8) * 2 + core, narrow)

    side = ((1 - y_lo) * 16 + z * 2 + core, narrow)
    twin = (y_lo * 16 + z * 2 + 1 - core, narrow)
    first_x, second_x = x + 1 - 2 * (x % 2), 3 - x
    bits = (((x + 1) // 2) % 2, x // 2)
    pairs = ((wide, y_hi * 4 + first_x), (wide, y_hi * 4 + second_x))
    across = (wide, (1 - y_hi) * 4 + x)
    diagonals = ((wide, (1 - y_hi) * 4 + first_x), (wide, (1 - y_hi) * 4 + second_x))

    loads = [
        pltpu.make_async_copy(source, target, load_sem.at[index])
        for index, (source, target) in enumerate(
            (
                (tokens, rows.at[OFFSETS.index(0) // 2, 0, OFFSETS.index(0) % 2, 0]),
                (gate_codes, gate_in),
                (up_codes, up_in),
                (down_codes, down_in),
            )
        )
    ]
    for load in loads:
        load.start()

    barrier = pltpu.get_barrier_semaphore()
    partners = [at_z(step) for step in OFFSETS if step]
    partners += [side, twin, across, *pairs, *diagonals]
    for partner in partners:
        pl.semaphore_signal(barrier, inc=1, device_id=partner, device_id_type=MESH)
    pl.semaphore_wait(barrier, len(partners))

    started = []

    def remote(source, target, device):
        index = len(started)
        copy = pltpu.make_async_remote_copy(
            src_ref=source, dst_ref=target,
            send_sem=send_sem.at[index], recv_sem=recv_sem.at[index],
            device_id=device, device_id_type=MESH,
        )
        copy.start()
        started.append(copy)
        return copy

    def shard(offset, other_core, other_side):
        slot = OFFSETS.index(offset)
        return rows.at[slot // 2, other_core, slot % 2, other_side]

    arrivals = {}

    def to_twin(offset, other_side):
        arrivals[offset, 1, other_side] = remote(
            shard(offset, 0, other_side), shard(offset, 1, other_side), twin
        )

    def to_other_side(offset):
        arrivals[offset, 0, 1] = [remote(shard(offset, 0, 0), shard(offset, 0, 1), side)]

    def take(offset, other_side):
        for copy in arrivals[offset, 0, other_side]:
            copy.wait_recv()
        to_twin(offset, other_side)

    middle = BLOCK * ((units // BLOCK + 1) // 2)
    streams = ((0, middle), (middle, units))

    def both(stream):
        start, end = streams[stream]
        return pl.ds(2 * start, 2 * (end - start))

    def widen(step, _):
        span = pl.ds(pl.multiple_of(step * BLOCK, BLOCK), BLOCK)
        for second, (codes, scale) in enumerate(((gate_in, gate_scale), (up_in, up_scale))):
            for start, end in streams:
                for at in range(start, end, BLOCK):
                    block = codes[span, at : at + BLOCK].astype(jnp.float32) * scale[at // BLOCK, step]
                    to = start + at + second * (end - start)
                    weight[span, to : to + BLOCK] = block.astype(jnp.bfloat16)
        return 0

    def widen_down(step, _):
        span = pl.ds(pl.multiple_of(step * BLOCK, BLOCK), BLOCK)
        for col in range(down.shape[1] // BLOCK):
            cut = slice(col * BLOCK, (col + 1) * BLOCK)
            block = down_in[span, cut].astype(jnp.float32) * down_scale[step, col]
            down[span, cut] = block.astype(jnp.bfloat16)
        return 0

    def span(start, size):
        return pl.ds(pl.multiple_of(start, SHARD), size)

    def lead(unit, stream):
        return (unit + stream) % 2

    def base(unit, stream):
        return unit * UNIT + bits[lead(unit, stream)] * QUARTER

    def within(unit, stream, other_x, other_y):
        follow = bits[1 - lead(unit, stream)]
        return (1 - follow if other_x else follow) * 32 + (1 - y_hi if other_y else y_hi) * SHARD

    def trio(unit, stream):
        follow = 1 - lead(unit, stream)
        return ((1, 0, pairs[follow]), (0, 1, across), (1, 1, diagonals[follow]))

    halves, quarters, gathers, forwards = {}, {}, {}, {}

    def multiply(unit):
        for offset in OFFSETS[2 * unit : 2 * unit + 2]:
            arrivals[offset, 1, 0].wait_recv()
            arrivals[offset, 1, 1].wait_recv()

        for stream in range(2):
            cut = both(stream)
            sums[pl.ds(unit * UNIT, UNIT), cut] = jnp.dot(
                rows[unit].reshape(UNIT, rows.shape[-1]), weight[:, cut],
                preferred_element_type=jnp.float32,
            )
            away = unit * UNIT + (1 - bits[lead(unit, stream)]) * QUARTER
            send1[unit, :, cut] = sums[span(away, QUARTER), cut].astype(jnp.bfloat16)
            halves[unit, stream] = remote(
                send1.at[unit, :, cut], recv1.at[unit, :, cut], pairs[lead(unit, stream)]
            )

    def partial(unit, stream, other_x, other_y):
        inner, cut = within(unit, stream, other_x, other_y), both(stream)
        return sums[span(base(unit, stream) + inner, SHARD), cut] + recv1[
            unit, span(inner, SHARD), cut
        ].astype(jnp.float32)

    def scatter(unit):
        for stream in range(2):
            halves[unit, stream].wait_recv()
            cut = both(stream)
            for index, (other_x, other_y, device) in enumerate(trio(unit, stream)):
                send2[unit, index, :, cut] = partial(unit, stream, other_x, other_y).astype(
                    jnp.bfloat16
                )
                quarters[unit, stream, index] = remote(
                    send2.at[unit, index, :, cut], recv2.at[unit, index, :, cut], device
                )

    def activate(unit):
        for stream, (start, end) in enumerate(streams):
            total = partial(unit, stream, 0, 0)
            for index in range(3):
                quarters[unit, stream, index].wait_recv()
                total = total + recv2[unit, index, :, both(stream)].astype(jnp.float32)
            gate, up = total[:, : end - start], total[:, end - start :]
            mine = span(base(unit, stream) + within(unit, stream, 0, 0), SHARD)
            hidden[mine, start:end] = (gate / (1.0 + jnp.exp(-gate)) * up).astype(jnp.bfloat16)
            piece = hidden.at[mine, pl.ds(start, end - start)]
            for index, (_, _, device) in enumerate(trio(unit, stream)):
                gathers[unit, stream, index] = remote(piece, piece, device)

    def forward(unit):
        for stream, (start, end) in enumerate(streams):
            for index in range(3):
                gathers[unit, stream, index].wait_recv()
            piece = hidden.at[span(base(unit, stream), QUARTER), pl.ds(start, end - start)]
            forwards[unit, stream] = remote(piece, piece, pairs[lead(unit, stream)])

    twins, sides, rings = {}, {}, {}

    def project(unit):
        for stream in range(2):
            forwards[unit, stream].wait_recv()

        half = down.shape[1] // 2
        twins[unit] = []
        for part in range(2):
            cut = pl.ds(part * half, half)
            outs[unit, :, cut] = jnp.dot(
                hidden[pl.ds(unit * UNIT, UNIT), :], down[:, cut],
                preferred_element_type=jnp.float32,
            )
            core_send[unit, :, cut] = outs[unit, QUARTER:, cut].astype(jnp.bfloat16)
            twins[unit].append(
                remote(core_send.at[unit, :, cut], core_recv.at[unit, :, cut], twin)
            )

    def paired(slot, other_side):
        at = pl.ds((slot % 2) * 32 + other_side * SHARD, SHARD)
        return outs[slot // 2, at, :] + core_recv[slot // 2, at, :].astype(jnp.float32)

    def to_side(unit):
        for copy in twins[unit]:
            copy.wait_recv()
        for slot in (2 * unit, 2 * unit + 1):
            side_send[slot] = paired(slot, 1).astype(jnp.bfloat16)
        cut = pl.ds(2 * unit, 2)
        sides[unit] = remote(side_send.at[cut], side_recv.at[cut], side)

    def local(slot):
        return paired(slot, 0) + side_recv[slot].astype(jnp.float32)

    def to_ring(unit):
        sides[unit].wait_recv()
        for slot in (2 * unit, 2 * unit + 1):
            if OFFSETS[slot]:
                ring_send[slot] = local(slot).astype(jnp.bfloat16)
                rings[slot] = remote(ring_send.at[slot], ring_recv.at[slot], at_z(OFFSETS[slot]))

    loads[0].wait()
    for offset in (1, -1):
        arrivals[offset, 0, 0] = [remote(shard(0, 0, 0), shard(offset, 0, 0), at_z(-offset))]
    to_other_side(0)
    for offset in (2, -2):
        arrivals[offset, 0, 0] = [remote(shard(0, 0, 0), shard(offset, 0, 0), at_z(-offset))]
    to_twin(0, 0)
    arrivals[4, 0, 0] = []
    steps = weight.shape[0] // BLOCK
    loads[1].wait()
    loads[2].wait()
    lax.fori_loop(0, steps // 4, widen, 0)
    take(0, 1)
    for offset in (1, -1):
        arrivals[offset, 0, 1] = [remote(shard(0, 0, 1), shard(offset, 0, 1), at_z(-offset))]
    take(1, 0)
    take(-1, 0)
    lax.fori_loop(steps // 4, steps // 2, widen, 0)
    half = tokens.shape[1] // 2
    for offset, sign, columns in ((2, 1, pl.ds(0, half)), (-2, -1, pl.ds(half, half))):
        take(offset, 0)
        here = shard(offset, 0, 0)
        arrivals[3 * sign, 0, 0] = [remote(here, shard(3 * sign, 0, 0), at_z(-sign))]
        arrivals[4, 0, 0].append(
            remote(here.at[:, columns], shard(4, 0, 0).at[:, columns], at_z(-2 * sign))
        )
        to_other_side(offset)
    lax.fori_loop(steps // 2, steps, widen, 0)
    take(1, 1)
    take(-1, 1)
    multiply(0)
    take(3, 0)
    to_other_side(3)
    take(2, 1)
    take(-3, 0)
    to_other_side(-3)
    take(-2, 1)
    take(4, 0)
    to_other_side(4)
    multiply(3)
    take(3, 1)
    take(-3, 1)
    loads[3].wait()
    lax.fori_loop(0, down.shape[0] // BLOCK, widen_down, 0)
    scatter(0)
    multiply(1)
    take(4, 1)
    scatter(3)
    multiply(2)
    activate(0)
    scatter(1)
    activate(3)
    scatter(2)
    forward(0)
    activate(1)
    forward(3)
    project(0)
    activate(2)
    to_side(0)
    forward(1)
    project(3)
    to_side(3)
    forward(2)
    project(1)
    to_ring(0)
    to_side(1)
    project(2)
    to_ring(3)
    to_side(2)
    to_ring(1)
    to_ring(2)
    total = local(OFFSETS.index(0))
    for slot, copy in rings.items():
        copy.wait_recv()
        total = total + ring_recv[slot].astype(jnp.float32)
    mixed[...] = total.astype(jnp.bfloat16)

    for copy in started:
        copy.wait_send()


def feed_forward(tokens, gate_codes, gate_scale, up_codes, up_scale, down_codes, down_scale):
    depth, units = gate_codes.shape
    bf16, f32 = jnp.bfloat16, jnp.float32
    any_space, scalars = pl.BlockSpec(memory_space=pl.ANY), pl.BlockSpec(memory_space=pltpu.SMEM)
    dma = pltpu.SemaphoreType.DMA
    return pl.pallas_call(
        kernel,
        out_shape=pltpu.VMEM(tokens.shape, bf16),
        in_specs=[any_space, any_space, scalars, any_space, scalars, any_space, scalars],
        out_specs=pl.BlockSpec(memory_space=pltpu.VMEM),
        scratch_shapes=[
            pltpu.VMEM((depth, units), bf16),
            pltpu.VMEM((depth, units), bf16),
            pltpu.VMEM((units, depth), bf16),
            pltpu.VMEM((depth, 2 * units), bf16),
            pltpu.VMEM((units, depth), bf16),
            pltpu.VMEM((UNITS, 2, 2, 2, SHARD, depth), bf16),
            pltpu.VMEM((UNITS * UNIT, 2 * units), f32),
            pltpu.VMEM((UNITS * UNIT, units), bf16),
            pltpu.VMEM((UNITS, UNIT, depth), f32),
            pltpu.VMEM((UNITS, QUARTER, 2 * units), bf16),
            pltpu.VMEM((UNITS, 3, SHARD, 2 * units), bf16),
            pltpu.VMEM((UNITS, QUARTER, 2 * units), bf16),
            pltpu.VMEM((UNITS, 3, SHARD, 2 * units), bf16),
            pltpu.VMEM((UNITS, QUARTER, depth), bf16),
            pltpu.VMEM((UNITS, QUARTER, depth), bf16),
            pltpu.VMEM((2 * UNITS, SHARD, depth), bf16),
            pltpu.VMEM((2 * UNITS, SHARD, depth), bf16),
            pltpu.VMEM((2 * UNITS, SHARD, depth), bf16),
            pltpu.VMEM((2 * UNITS, SHARD, depth), bf16),
            dma((4,)),
            dma((COPIES,)),
            dma((COPIES,)),
        ],
        compiler_params=pltpu.CompilerParams(
            collective_id=0, has_side_effects=True, vmem_limit_bytes=56 << 20
        ),
    )(tokens, gate_codes, gate_scale.T, up_codes, up_scale.T, down_codes, down_scale)


def solution(mesh):
    return jax.shard_map(
        feed_forward,
        mesh=mesh,
        in_specs=(
            P("wide", "narrow"),
            P("narrow", "wide"),
            P("narrow", "wide"),
            P("narrow", "wide"),
            P("narrow", "wide"),
            P("wide", "narrow"),
            P("wide", "narrow"),
        ),
        out_specs=P("wide", "narrow"),
        check_vma=False,
    )
```

```python
import jax
import jax.numpy as jnp
from jax import lax
from jax.experimental import pallas as pl
from jax.experimental.pallas import tpu as pltpu
from jax.sharding import PartitionSpec as P

MESH = pl.DeviceIdType.MESH
BLOCK = 128
SHARD = 16
UNITS = 4
UNIT = 128
QUARTER = 64
COPIES = 128
OFFSETS = (1, -1, 2, -2, 3, -3, 4, 0)


def kernel(
    tokens, gate_codes, gate_scale, up_codes, up_scale, down_codes, down_scale,
    mixed,
    gate_in, up_in, down_in, weight, down, rows, sums, hidden, outs,
    send1, send2, recv1, recv2,
    core_send, core_recv, side_send, side_recv, ring_send, ring_recv,
    load_sem, send_sem, recv_sem,
):
    wide, narrow = lax.axis_index("wide"), lax.axis_index("narrow")
    y_lo, z, core, y_hi, x = wide // 16, (wide // 2) % 8, wide % 2, narrow // 4, narrow % 4
    units = gate_codes.shape[1]

    def at_z(step):
        return (y_lo * 16 + ((z + step + 8) % 8) * 2 + core, narrow)

    side = ((1 - y_lo) * 16 + z * 2 + core, narrow)
    twin = (y_lo * 16 + z * 2 + 1 - core, narrow)
    first_x, second_x = x + 1 - 2 * (x % 2), 3 - x
    bits = (((x + 1) // 2) % 2, x // 2)
    pairs = ((wide, y_hi * 4 + first_x), (wide, y_hi * 4 + second_x))
    across = (wide, (1 - y_hi) * 4 + x)
    diagonals = ((wide, (1 - y_hi) * 4 + first_x), (wide, (1 - y_hi) * 4 + second_x))

    loads = [
        pltpu.make_async_copy(source, target, load_sem.at[index])
        for index, (source, target) in enumerate(
            (
                (tokens, rows.at[OFFSETS.index(0) // 2, 0, OFFSETS.index(0) % 2, 0]),
                (gate_codes, gate_in),
                (up_codes, up_in),
                (down_codes, down_in),
            )
        )
    ]
    for load in loads:
        load.start()

    barrier = pltpu.get_barrier_semaphore()
    partners = [at_z(step) for step in (1, -1, 2, -2)]
    partners += [side, twin, across, *pairs, *diagonals]
    for partner in partners:
        pl.semaphore_signal(barrier, inc=1, device_id=partner, device_id_type=MESH)
    pl.semaphore_wait(barrier, len(partners))

    started = []

    def remote(source, target, device):
        index = len(started)
        copy = pltpu.make_async_remote_copy(
            src_ref=source, dst_ref=target,
            send_sem=send_sem.at[index], recv_sem=recv_sem.at[index],
            device_id=device, device_id_type=MESH,
        )
        copy.start()
        started.append(copy)
        return copy

    def shard(offset, other_core, other_side):
        slot = OFFSETS.index(offset)
        return rows.at[slot // 2, other_core, slot % 2, other_side]

    arrivals = {}

    def to_twin(offset, other_side):
        arrivals[offset, 1, other_side] = remote(
            shard(offset, 0, other_side), shard(offset, 1, other_side), twin
        )

    def to_other_side(offset):
        arrivals[offset, 0, 1] = [remote(shard(offset, 0, 0), shard(offset, 0, 1), side)]

    def take(offset, other_side):
        for copy in arrivals[offset, 0, other_side]:
            copy.wait_recv()
        to_twin(offset, other_side)

    middle = BLOCK * ((units // BLOCK + 1) // 2)
    streams = ((0, middle), (middle, units))

    def both(stream):
        start, end = streams[stream]
        return pl.ds(2 * start, 2 * (end - start))

    def widen(step, _):
        span = pl.ds(pl.multiple_of(step * BLOCK, BLOCK), BLOCK)
        for second, (codes, scale) in enumerate(((gate_in, gate_scale), (up_in, up_scale))):
            for start, end in streams:
                for at in range(start, end, BLOCK):
                    block = codes[span, at : at + BLOCK].astype(jnp.float32) * scale[at // BLOCK, step]
                    to = start + at + second * (end - start)
                    weight[span, to : to + BLOCK] = block.astype(jnp.bfloat16)
        return 0

    def widen_down(step, _):
        span = pl.ds(pl.multiple_of(step * BLOCK, BLOCK), BLOCK)
        for col in range(down.shape[1] // BLOCK):
            cut = slice(col * BLOCK, (col + 1) * BLOCK)
            block = down_in[span, cut].astype(jnp.float32) * down_scale[step, col]
            down[span, cut] = block.astype(jnp.bfloat16)
        return 0

    def span(start, size):
        return pl.ds(pl.multiple_of(start, SHARD), size)

    def lead(unit, stream):
        return (unit + stream) % 2

    def base(unit, stream):
        return unit * UNIT + bits[lead(unit, stream)] * QUARTER

    def within(unit, stream, other_x, other_y):
        follow = bits[1 - lead(unit, stream)]
        return (1 - follow if other_x else follow) * 32 + (1 - y_hi if other_y else y_hi) * SHARD

    def trio(unit, stream):
        follow = 1 - lead(unit, stream)
        return ((1, 0, pairs[follow]), (0, 1, across), (1, 1, diagonals[follow]))

    halves, quarters, gathers, forwards = {}, {}, {}, {}

    def multiply(unit):
        for offset in OFFSETS[2 * unit : 2 * unit + 2]:
            arrivals[offset, 1, 0].wait_recv()
            arrivals[offset, 1, 1].wait_recv()

        for stream in range(2):
            cut = both(stream)
            sums[pl.ds(unit * UNIT, UNIT), cut] = jnp.dot(
                rows[unit].reshape(UNIT, rows.shape[-1]), weight[:, cut],
                preferred_element_type=jnp.float32,
            )
            away = unit * UNIT + (1 - bits[lead(unit, stream)]) * QUARTER
            send1[unit, :, cut] = sums[span(away, QUARTER), cut].astype(jnp.bfloat16)
            halves[unit, stream] = remote(
                send1.at[unit, :, cut], recv1.at[unit, :, cut], pairs[lead(unit, stream)]
            )

    def partial(unit, stream, other_x, other_y):
        inner, cut = within(unit, stream, other_x, other_y), both(stream)
        return sums[span(base(unit, stream) + inner, SHARD), cut] + recv1[
            unit, span(inner, SHARD), cut
        ].astype(jnp.float32)

    def scatter(unit):
        for stream in range(2):
            halves[unit, stream].wait_recv()
            cut = both(stream)
            for index, (other_x, other_y, device) in enumerate(trio(unit, stream)):
                send2[unit, index, :, cut] = partial(unit, stream, other_x, other_y).astype(
                    jnp.bfloat16
                )
                quarters[unit, stream, index] = remote(
                    send2.at[unit, index, :, cut], recv2.at[unit, index, :, cut], device
                )

    def activate(unit):
        for stream, (start, end) in enumerate(streams):
            total = partial(unit, stream, 0, 0)
            for index in range(3):
                quarters[unit, stream, index].wait_recv()
                total = total + recv2[unit, index, :, both(stream)].astype(jnp.float32)
            gate, up = total[:, : end - start], total[:, end - start :]
            mine = span(base(unit, stream) + within(unit, stream, 0, 0), SHARD)
            hidden[mine, start:end] = (gate / (1.0 + jnp.exp(-gate)) * up).astype(jnp.bfloat16)
            piece = hidden.at[mine, pl.ds(start, end - start)]
            for index, (_, _, device) in enumerate(trio(unit, stream)):
                gathers[unit, stream, index] = remote(piece, piece, device)

    def forward(unit):
        for stream, (start, end) in enumerate(streams):
            for index in range(3):
                gathers[unit, stream, index].wait_recv()
            piece = hidden.at[span(base(unit, stream), QUARTER), pl.ds(start, end - start)]
            forwards[unit, stream] = remote(piece, piece, pairs[lead(unit, stream)])

    twins, sides, rings = {}, {}, {}

    def project(unit):
        for stream in range(2):
            forwards[unit, stream].wait_recv()

        half = down.shape[1] // 2
        twins[unit] = []
        for part in range(2):
            cut = pl.ds(part * half, half)
            outs[unit, :, cut] = jnp.dot(
                hidden[pl.ds(unit * UNIT, UNIT), :], down[:, cut],
                preferred_element_type=jnp.float32,
            )
            core_send[unit, :, cut] = outs[unit, QUARTER:, cut].astype(jnp.bfloat16)
            twins[unit].append(
                remote(core_send.at[unit, :, cut], core_recv.at[unit, :, cut], twin)
            )

    def paired(slot, other_side):
        at = pl.ds((slot % 2) * 32 + other_side * SHARD, SHARD)
        return outs[slot // 2, at, :] + core_recv[slot // 2, at, :].astype(jnp.float32)

    def to_side(unit):
        for copy in twins[unit]:
            copy.wait_recv()
        for slot in (2 * unit, 2 * unit + 1):
            side_send[slot] = paired(slot, 1).astype(jnp.bfloat16)
        cut = pl.ds(2 * unit, 2)
        sides[unit] = remote(side_send.at[cut], side_recv.at[cut], side)

    def local(slot):
        return paired(slot, 0) + side_recv[slot].astype(jnp.float32)

    def to_ring(unit):
        sides[unit].wait_recv()
        for slot in (2 * unit, 2 * unit + 1):
            if OFFSETS[slot]:
                ring_send[slot] = local(slot).astype(jnp.bfloat16)
                rings[slot] = remote(ring_send.at[slot], ring_recv.at[slot], at_z(OFFSETS[slot]))

    loads[0].wait()
    for offset in (1, -1):
        arrivals[offset, 0, 0] = [remote(shard(0, 0, 0), shard(offset, 0, 0), at_z(-offset))]
    to_other_side(0)
    for offset in (2, -2):
        arrivals[offset, 0, 0] = [remote(shard(0, 0, 0), shard(offset, 0, 0), at_z(-offset))]
    to_twin(0, 0)
    arrivals[4, 0, 0] = []
    steps = weight.shape[0] // BLOCK
    loads[1].wait()
    loads[2].wait()
    lax.fori_loop(0, steps // 4, widen, 0)
    take(0, 1)
    for offset in (1, -1):
        arrivals[offset, 0, 1] = [remote(shard(0, 0, 1), shard(offset, 0, 1), at_z(-offset))]
    take(1, 0)
    take(-1, 0)
    lax.fori_loop(steps // 4, steps // 2, widen, 0)
    half = tokens.shape[1] // 2
    for offset, sign, columns in ((2, 1, pl.ds(0, half)), (-2, -1, pl.ds(half, half))):
        take(offset, 0)
        here = shard(offset, 0, 0)
        arrivals[3 * sign, 0, 0] = [remote(here, shard(3 * sign, 0, 0), at_z(-sign))]
        arrivals[4, 0, 0].append(
            remote(here.at[:, columns], shard(4, 0, 0).at[:, columns], at_z(-2 * sign))
        )
        to_other_side(offset)
    lax.fori_loop(steps // 2, steps, widen, 0)
    take(1, 1)
    take(-1, 1)
    multiply(0)
    take(-3, 0)
    to_other_side(-3)
    take(-2, 1)
    take(3, 0)
    to_other_side(3)
    take(2, 1)
    multiply(1)
    take(-3, 1)
    take(4, 0)
    to_other_side(4)
    loads[3].wait()
    lax.fori_loop(0, down.shape[0] // BLOCK, widen_down, 0)
    scatter(0)
    take(3, 1)
    multiply(2)
    take(4, 1)
    scatter(1)
    multiply(3)
    activate(0)
    scatter(2)
    activate(1)
    scatter(3)
    forward(0)
    activate(2)
    forward(1)
    project(0)
    activate(3)
    to_side(0)
    forward(2)
    project(1)
    to_side(1)
    forward(3)
    project(2)
    to_ring(0)
    to_side(2)
    project(3)
    to_ring(1)
    to_side(3)
    to_ring(2)
    to_ring(3)
    total = local(OFFSETS.index(0))
    for slot, copy in rings.items():
        copy.wait_recv()
        total = total + ring_recv[slot].astype(jnp.float32)
    mixed[...] = total.astype(jnp.bfloat16)

    for copy in started:
        copy.wait_send()


def feed_forward(tokens, gate_codes, gate_scale, up_codes, up_scale, down_codes, down_scale):
    depth, units = gate_codes.shape
    bf16, f32 = jnp.bfloat16, jnp.float32
    any_space, scalars = pl.BlockSpec(memory_space=pl.ANY), pl.BlockSpec(memory_space=pltpu.SMEM)
    dma = pltpu.SemaphoreType.DMA
    return pl.pallas_call(
        kernel,
        out_shape=pltpu.VMEM(tokens.shape, bf16),
        in_specs=[any_space, any_space, scalars, any_space, scalars, any_space, scalars],
        out_specs=pl.BlockSpec(memory_space=pltpu.VMEM),
        scratch_shapes=[
            pltpu.VMEM((depth, units), bf16),
            pltpu.VMEM((depth, units), bf16),
            pltpu.VMEM((units, depth), bf16),
            pltpu.VMEM((depth, 2 * units), bf16),
            pltpu.VMEM((units, depth), bf16),
            pltpu.VMEM((UNITS, 2, 2, 2, SHARD, depth), bf16),
            pltpu.VMEM((UNITS * UNIT, 2 * units), f32),
            pltpu.VMEM((UNITS * UNIT, units), bf16),
            pltpu.VMEM((UNITS, UNIT, depth), f32),
            pltpu.VMEM((UNITS, QUARTER, 2 * units), bf16),
            pltpu.VMEM((UNITS, 3, SHARD, 2 * units), bf16),
            pltpu.VMEM((UNITS, QUARTER, 2 * units), bf16),
            pltpu.VMEM((UNITS, 3, SHARD, 2 * units), bf16),
            pltpu.VMEM((UNITS, QUARTER, depth), bf16),
            pltpu.VMEM((UNITS, QUARTER, depth), bf16),
            pltpu.VMEM((2 * UNITS, SHARD, depth), bf16),
            pltpu.VMEM((2 * UNITS, SHARD, depth), bf16),
            pltpu.VMEM((2 * UNITS, SHARD, depth), bf16),
            pltpu.VMEM((2 * UNITS, SHARD, depth), bf16),
            dma((4,)),
            dma((COPIES,)),
            dma((COPIES,)),
        ],
        compiler_params=pltpu.CompilerParams(
            collective_id=0, has_side_effects=True, vmem_limit_bytes=56 << 20
        ),
    )(tokens, gate_codes, gate_scale.T, up_codes, up_scale.T, down_codes, down_scale)


def solution(mesh):
    return jax.shard_map(
        feed_forward,
        mesh=mesh,
        in_specs=(
            P("wide", "narrow"),
            P("narrow", "wide"),
            P("narrow", "wide"),
            P("narrow", "wide"),
            P("narrow", "wide"),
            P("wide", "narrow"),
            P("wide", "narrow"),
        ),
        out_specs=P("wide", "narrow"),
        check_vma=False,
    )
```

```python
import jax
import jax.numpy as jnp
from jax import lax
from jax.experimental import pallas as pl
from jax.experimental.pallas import tpu as pltpu
from jax.sharding import PartitionSpec as P

MESH = pl.DeviceIdType.MESH
BLOCK = 128
SHARD = 16
UNITS = 4
UNIT = 128
QUARTER = 64
COPIES = 128
OFFSETS = (1, -1, 2, -2, 3, -3, 4, 0)


def kernel(
    tokens, gate_codes, gate_scale, up_codes, up_scale, down_codes, down_scale,
    mixed,
    gate_in, up_in, down_in, weight, down, rows, sums, hidden, outs,
    send1, send2, recv1, recv2,
    core_send, core_recv, side_send, side_recv, ring_send, ring_recv,
    load_sem, send_sem, recv_sem,
):
    wide, narrow = lax.axis_index("wide"), lax.axis_index("narrow")
    y_lo, z, core, y_hi, x = wide // 16, (wide // 2) % 8, wide % 2, narrow // 4, narrow % 4
    units = gate_codes.shape[1]

    def at_z(step):
        return (y_lo * 16 + ((z + step + 8) % 8) * 2 + core, narrow)

    side = ((1 - y_lo) * 16 + z * 2 + core, narrow)
    twin = (y_lo * 16 + z * 2 + 1 - core, narrow)
    first_x, second_x = x + 1 - 2 * (x % 2), 3 - x
    bits = (((x + 1) // 2) % 2, x // 2)
    pairs = ((wide, y_hi * 4 + first_x), (wide, y_hi * 4 + second_x))
    across = (wide, (1 - y_hi) * 4 + x)
    diagonals = ((wide, (1 - y_hi) * 4 + first_x), (wide, (1 - y_hi) * 4 + second_x))

    loads = [
        pltpu.make_async_copy(source, target, load_sem.at[index])
        for index, (source, target) in enumerate(
            (
                (tokens, rows.at[OFFSETS.index(0) // 2, 0, OFFSETS.index(0) % 2, 0]),
                (gate_codes, gate_in),
                (up_codes, up_in),
                (down_codes, down_in),
            )
        )
    ]
    for load in loads:
        load.start()

    barrier = pltpu.get_barrier_semaphore()
    partners = [at_z(step) for step in (1, -1, 2, -2)]
    partners += [side, twin, across, *pairs]
    for partner in partners:
        pl.semaphore_signal(barrier, inc=1, device_id=partner, device_id_type=MESH)
    pl.semaphore_wait(barrier, len(partners))

    started = []

    def remote(source, target, device):
        index = len(started)
        copy = pltpu.make_async_remote_copy(
            src_ref=source, dst_ref=target,
            send_sem=send_sem.at[index], recv_sem=recv_sem.at[index],
            device_id=device, device_id_type=MESH,
        )
        copy.start()
        started.append(copy)
        return copy

    def shard(offset, other_core, other_side):
        slot = OFFSETS.index(offset)
        return rows.at[slot // 2, other_core, slot % 2, other_side]

    arrivals = {}

    def to_twin(offset, other_side):
        arrivals[offset, 1, other_side] = remote(
            shard(offset, 0, other_side), shard(offset, 1, other_side), twin
        )

    def to_other_side(offset):
        arrivals[offset, 0, 1] = [remote(shard(offset, 0, 0), shard(offset, 0, 1), side)]

    def take(offset, other_side):
        for copy in arrivals[offset, 0, other_side]:
            copy.wait_recv()
        to_twin(offset, other_side)

    middle = BLOCK * ((units // BLOCK + 1) // 2)
    streams = ((0, middle), (middle, units))

    def both(stream):
        start, end = streams[stream]
        return pl.ds(2 * start, 2 * (end - start))

    def widen(step, _):
        span = pl.ds(pl.multiple_of(step * BLOCK, BLOCK), BLOCK)
        for second, (codes, scale) in enumerate(((gate_in, gate_scale), (up_in, up_scale))):
            for start, end in streams:
                for at in range(start, end, BLOCK):
                    block = codes[span, at : at + BLOCK].astype(jnp.float32) * scale[at // BLOCK, step]
                    to = start + at + second * (end - start)
                    weight[span, to : to + BLOCK] = block.astype(jnp.bfloat16)
        return 0

    def widen_down(step, _):
        span = pl.ds(pl.multiple_of(step * BLOCK, BLOCK), BLOCK)
        for col in range(down.shape[1] // BLOCK):
            cut = slice(col * BLOCK, (col + 1) * BLOCK)
            block = down_in[span, cut].astype(jnp.float32) * down_scale[step, col]
            down[span, cut] = block.astype(jnp.bfloat16)
        return 0

    def span(start, size):
        return pl.ds(pl.multiple_of(start, SHARD), size)

    def lead(unit, stream):
        return (unit + stream) % 2

    def base(unit, stream):
        return unit * UNIT + bits[lead(unit, stream)] * QUARTER

    def within(unit, stream, other_x, other_y):
        follow = bits[1 - lead(unit, stream)]
        return (1 - follow if other_x else follow) * 32 + (1 - y_hi if other_y else y_hi) * SHARD

    def trio(unit, stream):
        follow = 1 - lead(unit, stream)
        return ((1, 0, pairs[follow]), (0, 1, across), (1, 1, diagonals[follow]))

    halves, quarters, gathers, forwards = {}, {}, {}, {}

    def multiply(unit):
        for offset in OFFSETS[2 * unit : 2 * unit + 2]:
            arrivals[offset, 1, 0].wait_recv()
            arrivals[offset, 1, 1].wait_recv()

        for stream in range(2):
            cut = both(stream)
            sums[pl.ds(unit * UNIT, UNIT), cut] = jnp.dot(
                rows[unit].reshape(UNIT, rows.shape[-1]), weight[:, cut],
                preferred_element_type=jnp.float32,
            )
            away = unit * UNIT + (1 - bits[lead(unit, stream)]) * QUARTER
            send1[unit, :, cut] = sums[span(away, QUARTER), cut].astype(jnp.bfloat16)
            halves[unit, stream] = remote(
                send1.at[unit, :, cut], recv1.at[unit, :, cut], pairs[lead(unit, stream)]
            )

    def partial(unit, stream, other_x, other_y):
        inner, cut = within(unit, stream, other_x, other_y), both(stream)
        return sums[span(base(unit, stream) + inner, SHARD), cut] + recv1[
            unit, span(inner, SHARD), cut
        ].astype(jnp.float32)

    def scatter(unit):
        for stream in range(2):
            halves[unit, stream].wait_recv()
        for stream in range(2):
            cut = both(stream)
            for index, (other_x, other_y, device) in enumerate(trio(unit, stream)):
                send2[unit, index, :, cut] = partial(unit, stream, other_x, other_y).astype(
                    jnp.bfloat16
                )
                quarters[unit, stream, index] = remote(
                    send2.at[unit, index, :, cut], recv2.at[unit, index, :, cut], device
                )

    def activate(unit):
        for stream, (start, end) in enumerate(streams):
            total = partial(unit, stream, 0, 0)
            for index in range(3):
                quarters[unit, stream, index].wait_recv()
                total = total + recv2[unit, index, :, both(stream)].astype(jnp.float32)
            gate, up = total[:, : end - start], total[:, end - start :]
            mine = span(base(unit, stream) + within(unit, stream, 0, 0), SHARD)
            hidden[mine, start:end] = (gate / (1.0 + jnp.exp(-gate)) * up).astype(jnp.bfloat16)
            piece = hidden.at[mine, pl.ds(start, end - start)]
            for index, (_, _, device) in enumerate(trio(unit, stream)):
                gathers[unit, stream, index] = remote(piece, piece, device)

    def forward(unit):
        for stream, (start, end) in enumerate(streams):
            for index in range(3):
                gathers[unit, stream, index].wait_recv()
            piece = hidden.at[span(base(unit, stream), QUARTER), pl.ds(start, end - start)]
            forwards[unit, stream] = remote(piece, piece, pairs[lead(unit, stream)])

    twins, sides, rings = {}, {}, {}

    def project(unit):
        for stream in range(2):
            forwards[unit, stream].wait_recv()

        half = down.shape[1] // 2
        twins[unit] = []
        for part in range(2):
            cut = pl.ds(part * half, half)
            outs[unit, :, cut] = jnp.dot(
                hidden[pl.ds(unit * UNIT, UNIT), :], down[:, cut],
                preferred_element_type=jnp.float32,
            )
            core_send[unit, :, cut] = outs[unit, QUARTER:, cut].astype(jnp.bfloat16)
            twins[unit].append(
                remote(core_send.at[unit, :, cut], core_recv.at[unit, :, cut], twin)
            )

    def paired(slot, other_side):
        at = pl.ds((slot % 2) * 32 + other_side * SHARD, SHARD)
        return outs[slot // 2, at, :] + core_recv[slot // 2, at, :].astype(jnp.float32)

    def to_side(unit):
        for copy in twins[unit]:
            copy.wait_recv()
        for slot in (2 * unit, 2 * unit + 1):
            side_send[slot] = paired(slot, 1).astype(jnp.bfloat16)
        cut = pl.ds(2 * unit, 2)
        sides[unit] = remote(side_send.at[cut], side_recv.at[cut], side)

    def local(slot):
        return paired(slot, 0) + side_recv[slot].astype(jnp.float32)

    def to_ring(unit):
        sides[unit].wait_recv()
        for slot in (2 * unit, 2 * unit + 1):
            if OFFSETS[slot]:
                ring_send[slot] = local(slot).astype(jnp.bfloat16)
                rings[slot] = remote(ring_send.at[slot], ring_recv.at[slot], at_z(OFFSETS[slot]))

    loads[0].wait()
    for offset in (1, -1):
        arrivals[offset, 0, 0] = [remote(shard(0, 0, 0), shard(offset, 0, 0), at_z(-offset))]
    to_other_side(0)
    for offset in (2, -2):
        arrivals[offset, 0, 0] = [remote(shard(0, 0, 0), shard(offset, 0, 0), at_z(-offset))]
    to_twin(0, 0)
    arrivals[4, 0, 0] = []
    steps = weight.shape[0] // BLOCK
    loads[1].wait()
    loads[2].wait()
    lax.fori_loop(0, steps // 4, widen, 0)
    take(0, 1)
    for offset in (1, -1):
        arrivals[offset, 0, 1] = [remote(shard(0, 0, 1), shard(offset, 0, 1), at_z(-offset))]
    take(1, 0)
    take(-1, 0)
    lax.fori_loop(steps // 4, steps // 2, widen, 0)
    half = tokens.shape[1] // 2
    for offset, sign, columns in ((2, 1, pl.ds(0, half)), (-2, -1, pl.ds(half, half))):
        take(offset, 0)
        here = shard(offset, 0, 0)
        arrivals[3 * sign, 0, 0] = [remote(here, shard(3 * sign, 0, 0), at_z(-sign))]
        arrivals[4, 0, 0].append(
            remote(here.at[:, columns], shard(4, 0, 0).at[:, columns], at_z(-2 * sign))
        )
        to_other_side(offset)
    lax.fori_loop(steps // 2, steps, widen, 0)
    take(1, 1)
    take(-1, 1)
    multiply(0)
    take(-3, 0)
    to_other_side(-3)
    take(-2, 1)
    take(3, 0)
    to_other_side(3)
    take(2, 1)
    multiply(1)
    take(-3, 1)
    take(4, 0)
    to_other_side(4)
    loads[3].wait()
    lax.fori_loop(0, down.shape[0] // BLOCK, widen_down, 0)
    scatter(0)
    take(3, 1)
    multiply(2)
    take(4, 1)
    scatter(1)
    multiply(3)
    activate(0)
    scatter(2)
    activate(1)
    scatter(3)
    forward(0)
    activate(2)
    forward(1)
    project(0)
    activate(3)
    to_side(0)
    forward(2)
    project(1)
    to_side(1)
    forward(3)
    project(2)
    to_ring(0)
    to_side(2)
    project(3)
    to_ring(1)
    to_side(3)
    to_ring(2)
    to_ring(3)
    total = local(OFFSETS.index(0))
    for slot, copy in rings.items():
        copy.wait_recv()
        total = total + ring_recv[slot].astype(jnp.float32)
    mixed[...] = total.astype(jnp.bfloat16)

    for copy in started:
        copy.wait_send()


def feed_forward(tokens, gate_codes, gate_scale, up_codes, up_scale, down_codes, down_scale):
    depth, units = gate_codes.shape
    bf16, f32 = jnp.bfloat16, jnp.float32
    any_space, scalars = pl.BlockSpec(memory_space=pl.ANY), pl.BlockSpec(memory_space=pltpu.SMEM)
    dma = pltpu.SemaphoreType.DMA
    return pl.pallas_call(
        kernel,
        out_shape=pltpu.VMEM(tokens.shape, bf16),
        in_specs=[any_space, any_space, scalars, any_space, scalars, any_space, scalars],
        out_specs=pl.BlockSpec(memory_space=pltpu.VMEM),
        scratch_shapes=[
            pltpu.VMEM((depth, units), bf16),
            pltpu.VMEM((depth, units), bf16),
            pltpu.VMEM((units, depth), bf16),
            pltpu.VMEM((depth, 2 * units), bf16),
            pltpu.VMEM((units, depth), bf16),
            pltpu.VMEM((UNITS, 2, 2, 2, SHARD, depth), bf16),
            pltpu.VMEM((UNITS * UNIT, 2 * units), f32),
            pltpu.VMEM((UNITS * UNIT, units), bf16),
            pltpu.VMEM((UNITS, UNIT, depth), f32),
            pltpu.VMEM((UNITS, QUARTER, 2 * units), bf16),
            pltpu.VMEM((UNITS, 3, SHARD, 2 * units), bf16),
            pltpu.VMEM((UNITS, QUARTER, 2 * units), bf16),
            pltpu.VMEM((UNITS, 3, SHARD, 2 * units), bf16),
            pltpu.VMEM((UNITS, QUARTER, depth), bf16),
            pltpu.VMEM((UNITS, QUARTER, depth), bf16),
            pltpu.VMEM((2 * UNITS, SHARD, depth), bf16),
            pltpu.VMEM((2 * UNITS, SHARD, depth), bf16),
            pltpu.VMEM((2 * UNITS, SHARD, depth), bf16),
            pltpu.VMEM((2 * UNITS, SHARD, depth), bf16),
            dma((4,)),
            dma((COPIES,)),
            dma((COPIES,)),
        ],
        compiler_params=pltpu.CompilerParams(
            collective_id=0, has_side_effects=True, vmem_limit_bytes=56 << 20
        ),
    )(tokens, gate_codes, gate_scale.T, up_codes, up_scale.T, down_codes, down_scale)


def solution(mesh):
    return jax.shard_map(
        feed_forward,
        mesh=mesh,
        in_specs=(
            P("wide", "narrow"),
            P("narrow", "wide"),
            P("narrow", "wide"),
            P("narrow", "wide"),
            P("narrow", "wide"),
            P("wide", "narrow"),
            P("wide", "narrow"),
        ),
        out_specs=P("wide", "narrow"),
        check_vma=False,
    )
```
